128 devices in a mesh: dom: 32 (over z, y, core), grp: 4 (over x).
Axes of the slice: x: 4, y: 4, z: 4, core: 2. Of those that a mesh axis runs over, the one named last changes fastest.
Arguments:
- a_blocks: bfloat16 [128, 7, 48, 64, 448], P('dom', None, 'grp'), may hold values from -0.25 to 0.25
- prolong: bfloat16 [128, 7, 48, 64, 128], P('dom', None, 'grp'), may hold values from -0.75 to 0.75
- zagg: int32 [128], replicated, may hold values from 0 to 63, as said below
- xlen: int32 [4, 4], replicated, may hold values from 1 to 6, 12 in all within a row
Outputs:
- coarse_operator: bfloat16 [64, 16, 128, 640], P('dom', 'grp')
The draws below stay inside these ranges and needn't reach their ends.
Inputs may be any that keep to these rules, and one draw needn't show every extreme that they name: zagg starts at 0, never falls and rises by 0 or 1 from layer to layer; every run of 4 layers of one index of dom holds exactly 2 layers where a new interval begins, the first layer of all among them.
All inputs are finite; a program needn't handle non-finite values.
Results may differ from the reference program's by a relative error of at most 0.005.
Values may be sent and summed in bfloat16 or wider, within the bound.
A program may use at most 256 MiB of HBM per device.

```python
import math
import jax
import jax.numpy as jnp
import numpy as np
from jax import lax

B = 64
BC = 128
LX = 12
LY = 7
LZ = 4
NXI = 4
Z = 128
X = 48
N_DOM = 32
N_GRP = 4


def draw_zagg(key, part):
    noise = jax.random.randint(key, (N_DOM, LZ), 0, 1 << 20)
    places = jnp.arange(LZ, dtype=jnp.int32)
    scores = noise * LZ + places[None, :]
    marker = jnp.zeros((N_DOM, LZ), jnp.int32).at[0, 0].set(1)
    scores = jnp.where(marker > 0, -1, scores)
    ranking = jnp.argsort(jnp.argsort(scores, axis=1), axis=1)
    begins = (ranking < LZ // 2).astype(jnp.int32).reshape(-1)
    return (jnp.cumsum(begins) - 1).astype(jnp.int32)


def shard_levels(key, shape, shards, least, largest):
    def one(axis_at, blocks):
        heights = jax.random.uniform(jax.random.fold_in(jax.random.fold_in(key, 6), axis_at), (blocks,), jnp.float32, least / len(shards), largest / len(shards))
        return jnp.repeat(jnp.exp(heights), shape[axis_at] // blocks).reshape((-1,) + (1,) * (len(shape) - axis_at - 1))

    factor_of = one(*shards[0])
    for cut in shards[1:]:
        factor_of = factor_of * one(*cut)
    return factor_of


def length_profile(number_of, total, bound, skew):
    portions = [(1 << 20) // math.isqrt(grade ** skew) + 1 for grade in range(2, number_of + 1)]
    rest, counts = total - bound - (number_of - 1), [1] * (number_of - 1)
    while rest > 0:
        free = [i for i in range(number_of - 1) if counts[i] < bound]
        whole, budget = sum([portions[i] for i in free]), rest
        for i in free:
            addition = min(bound - counts[i], max(1, budget * portions[i] // whole), rest)
            counts[i] = counts[i] + addition
            rest = rest - addition
    return np.array([bound] + counts)


def ragged_sizes(stream_key, number_of, total, limit, slope):
    if number_of == 2:
        one = jax.random.randint(stream_key, (), max(1, total - limit), min(limit, total - 1) + 1)
        return jnp.stack([one, total - one])
    sizes = jnp.asarray(length_profile(number_of, total, limit, slope), jnp.int32)
    pairs = (number_of - 1) // 2
    donor, receiver = sizes[1:1 + 2 * pairs:2], sizes[2:2 + 2 * pairs:2]
    slack = jnp.minimum(donor - 1, limit - receiver)
    passed = jax.random.randint(jax.random.fold_in(stream_key, 1), (pairs,), 0, 1 << 20) % (slack + 1)
    sizes = sizes.at[1:1 + 2 * pairs:2].set(donor - passed).at[2:2 + 2 * pairs:2].set(receiver + passed)
    return sizes[jax.random.permutation(jax.random.fold_in(stream_key, 2), number_of)]


def gaussian(key, dims, scale, most, shards=(), kind=jnp.bfloat16):
    factor_of = shard_levels(key, dims, shards, -0.22, 0.18) if shards else 1.0
    result = jax.random.normal(key, dims, jnp.float32) * scale * factor_of
    return jnp.minimum(jnp.maximum(result, -most), most).astype(kind)


def setup_inputs(seed: int = 0) -> dict:
    keys = jax.random.split(jax.random.key(seed), 5)
    a_blocks = gaussian(keys[0], (Z, LY, X, B, 7 * B), (7 * B) ** -0.5, 0.25, ((0, 32), (2, 4)))
    prolong = gaussian(keys[1], (Z, LY, X, B, BC), B ** -0.5, 0.75, ((0, 32), (2, 4)))
    zagg = draw_zagg(jax.random.fold_in(keys[4], 71), 0)
    xlen = jax.vmap(lambda own: ragged_sizes(own, NXI, LX, LX // 3 + 2, 2))(jax.random.split(keys[3], N_GRP)).reshape((N_GRP, NXI)).astype(jnp.int32)
    return {"a_blocks": a_blocks, "prolong": prolong, "zagg": zagg, "xlen": xlen}


def reference(a_blocks, prolong, zagg, xlen):
    ends = jnp.cumsum(xlen, axis=1)
    columns = jnp.arange(LX, dtype=jnp.int32)
    within = jnp.sum((ends[:, :, None] <= columns[None, None, :]).astype(jnp.int32), axis=1)
    offsets = jnp.arange(N_GRP, dtype=jnp.int32)[:, None] * NXI
    xagg = (within + offsets).reshape(X).astype(jnp.int32)
    onehot = (xagg[None, :] == jnp.arange(NXI * N_GRP, dtype=jnp.int32)[:, None]).astype(jnp.float32)
    column_pad = jnp.pad(xagg, 1, constant_values=-1)
    same_xm = (column_pad[:-2] == xagg).astype(jnp.float32)[None, :, None, None]
    same_xp = (column_pad[2:] == xagg).astype(jnp.float32)[None, :, None, None]
    layer_pad = jnp.pad(zagg, 1, constant_values=-1)
    padded = jnp.pad(prolong, ((1, 1), (1, 1), (1, 1), (0, 0), (0, 0)))

    def one_layer(running, layer):
        coupling = lax.dynamic_index_in_dim(a_blocks, layer, 0, keepdims=False).astype(jnp.float32)
        window = lax.dynamic_slice_in_dim(padded, layer, 3, 0).astype(jnp.float32)
        centre = window[1, 1:-1, 1:-1]
        beside = [centre, window[1, 1:-1, :-2], window[1, 1:-1, 2:], window[1, :-2, 1:-1],
                  window[1, 2:, 1:-1], window[0, 1:-1, 1:-1], window[2, 1:-1, 1:-1]]
        products = [jnp.einsum('yxrs,yxsc->yxrc', coupling[..., k * B:(k + 1) * B], beside[k])
                    for k in range(7)]
        interval = layer_pad[layer + 1]
        same_zm = (layer_pad[layer] == interval).astype(jnp.float32)
        same_zp = (layer_pad[layer + 2] == interval).astype(jnp.float32)
        self_sum = (products[0] + products[3] + products[4] + same_xm * products[1]
                    + same_xp * products[2] + same_zm * products[5] + same_zp * products[6])
        slots = [self_sum, (1.0 - same_xm) * products[1], (1.0 - same_xp) * products[2],
                 (1.0 - same_zm) * products[5], (1.0 - same_zp) * products[6]]
        routed = jnp.concatenate(slots, axis=-1).astype(jnp.bfloat16).astype(jnp.float32)
        partial_sum = jnp.einsum('yxrc,yxrk->xck', centre, routed)
        coarse = jnp.einsum('ex,xck->eck', onehot, partial_sum, precision=lax.Precision.HIGHEST)
        current = lax.dynamic_index_in_dim(running, interval, 0, keepdims=True)
        running = lax.dynamic_update_index_in_dim(running, current + coarse[None], interval, 0)
        return running, None

    start = jnp.zeros((Z // 2, NXI * N_GRP, BC, 5 * BC), jnp.float32)
    running, _ = lax.scan(one_layer, start, jnp.arange(Z, dtype=jnp.int32))
    return running.astype(jnp.bfloat16)
```

```python
import functools

import jax
import jax.numpy as jnp
from jax import lax
from jax.experimental import pallas as pl
from jax.experimental.pallas import tpu as pltpu
from jax.sharding import PartitionSpec as P

BF = jnp.bfloat16
F32 = jnp.float32
UNROLL = 4


def product(lhs, rhs):
    return jnp.dot(lhs, rhs, preferred_element_type=F32)


def kernel(
    n_dom, n_grp, zagg, xlen, a_hbm, p_hbm, out_hbm,
    a, p, pt, rt, ert, v, ev, xv, below, above, left, right,
    carry_out, carry_in, last, done,
    a_sem, p_sem, z_send, z_recv, x_send, x_recv, c_send, c_recv, o_sem,
):
    layers, depth, columns, block, width = p.shape
    chunk = columns // 3
    intervals = xlen.shape[1]
    dom, grp = lax.axis_index("dom"), lax.axis_index("grp")
    has_below, has_above = dom > 0, dom < n_dom - 1
    has_left, has_right = grp > 0, grp < n_grp - 1
    MESH = pl.DeviceIdType.MESH
    sides = (
        (has_below, (dom - 1, grp)),
        (has_above, (dom + 1, grp)),
        (has_left, (dom, grp - 1)),
        (has_right, (dom, grp + 1)),
    )

    def part(ref, z, third):
        return ref.at[z, :, pl.ds(third * chunk, chunk)]

    a_copies = [
        [pltpu.make_async_copy(part(a_hbm, z, t), part(a, z, t), a_sem.at[z, t]) for t in range(3)]
        for z in range(layers)
    ]
    p_copies = [pltpu.make_async_copy(p_hbm.at[z], p.at[z], p_sem.at[z]) for z in range(layers)]
    p_copies[0].start()
    a_copies[0][0].start()
    p_copies[1].start()
    a_copies[0][1].start()
    a_copies[0][2].start()
    for z in range(1, layers):
        if z + 1 < layers:
            p_copies[z + 1].start()
        for t in range(3):
            a_copies[z][t].start()

    barrier = pltpu.get_barrier_semaphore()
    for there, device in sides:
        @pl.when(there)
        def _(device=device):
            pl.semaphore_signal(barrier, inc=1, device_id=device, device_id_type=MESH)
    pl.semaphore_wait(barrier, sum(jnp.where(there, 1, 0).astype(jnp.int32) for there, _ in sides))

    def remote(src, dst, send, recv, device):
        return pltpu.make_async_remote_copy(
            src_ref=src, dst_ref=dst, send_sem=send, recv_sem=recv,
            device_id=device, device_id_type=MESH,
        )

    def thirds(ref, t):
        return ref.at[:, pl.ds(t * chunk, chunk)]

    up = [
        remote(part(p_hbm, layers - 1, t), thirds(below, t), z_send.at[0, t], z_recv.at[0, t], (dom + 1, grp))
        for t in range(3)
    ]
    down = [
        remote(part(p_hbm, 0, t), thirds(above, t), z_send.at[1, t], z_recv.at[1, t], (dom - 1, grp))
        for t in range(3)
    ]
    rightward = remote(p_hbm.at[:, :, columns - 1], left, x_send.at[0], x_recv.at[0], (dom, grp + 1))
    leftward = remote(p_hbm.at[:, :, 0], right, x_send.at[1], x_recv.at[1], (dom, grp - 1))
    carry = remote(carry_out, carry_in, c_send, c_recv, (dom - 1, grp))

    @pl.when(has_above)
    def _():
        for t in range(3):
            up[t].start()

    @pl.when(has_below)
    def _():
        for t in range(3):
            down[t].start()

    @pl.when(has_right)
    def _():
        rightward.start()

    @pl.when(has_left)
    def _():
        leftward.start()

    for there, ref in ((has_below, below), (has_above, above), (has_left, left), (has_right, right), (has_above, carry_in)):
        @pl.when(jnp.logical_not(there))
        def _(ref=ref):
            for first in range(ref.shape[0]):
                ref[first] = jnp.zeros(ref.shape[1:], ref.dtype)

    one, none = jnp.int32(1), jnp.int32(0)

    def begins_at(layer):
        at = dom * layers + layer
        inner = jnp.where(
            zagg[jnp.minimum(at, n_dom * layers - 1)] != zagg[jnp.maximum(at - 1, 0)], one, none
        )
        return jnp.where(jnp.logical_or(at == 0, at == n_dom * layers), one, inner)

    begins = [begins_at(layer) for layer in range(layers + 1)]
    group = [begins[0]]
    for layer in range(1, layers):
        group.append(group[-1] + begins[layer])
    cuts = [none]
    for i in range(intervals):
        cuts.append(cuts[-1] + xlen[grp, i])

    def column_begins(x):
        found = none
        for i in range(intervals):
            found = jnp.where(x == cuts[i], one, found)
        return jnp.where(x == columns, one, found)

    def real(flag):
        return flag.astype(F32)

    rows = [slice(y * block, (y + 1) * block) for y in range(depth)]

    def main(z):
        low, high = z > 0, z < layers - 1
        slots = width * (1 + low + high)

        def first(x, slot):
            same_xm = (1.0 - real(column_begins(x))).astype(BF)
            same_xp = (1.0 - real(column_begins(x + 1))).astype(BF)
            xm, xp = jnp.maximum(x - 1, 0), jnp.minimum(x + 1, columns - 1)
            zero = jnp.zeros((block, width), BF)
            for y in range(depth):
                stack = jnp.concatenate(
                    [
                        p[z, y, x],
                        p[z, y, xm] * same_xm,
                        p[z, y, xp] * same_xp,
                        p[z, y - 1, x] if y > 0 else zero,
                        p[z, y + 1, x] if y < depth - 1 else zero,
                    ],
                    axis=0,
                )
                rt[slot, rows[y], 0:width] = product(a[z, y, x, :, 0 : 5 * block], stack).astype(BF)
                at = width
                if high:
                    rt[slot, rows[y], at : at + width] = product(
                        a[z, y, x, :, 6 * block : 7 * block], p[z + 1, y, x]
                    ).astype(BF)
                    at += width
                if low:
                    rt[slot, rows[y], at : at + width] = product(
                        a[z, y, x, :, 5 * block : 6 * block], p[z - 1, y, x]
                    ).astype(BF)

        def second(x, slot):
            turned = jnp.concatenate([p[z, y, x] for y in range(depth)], axis=0).T
            pt[z, x] = turned
            coarse = product(turned, rt[slot, :, 0:slots])
            before = v[z, jnp.maximum(x - 1, 0), :, 0:slots]
            v[z, x, :, 0:slots] = coarse + jnp.where(column_begins(x) == 1, 0.0, before)

        def step(j, _):
            for u in range(UNROLL):
                first(j * UNROLL + u, u)
                if u > 0:
                    second(j * UNROLL + u - 1, u - 1)
            second(j * UNROLL + UNROLL - 1, UNROLL - 1)
            return 0

        lax.fori_loop(0, columns // UNROLL, step, 0)

    def inside_columns(z):
        for i in range(1, intervals):
            hi = jnp.clip(cuts[i], 1, columns - 1)
            lo = hi - 1
            for y in range(depth):
                ert[0, rows[y]] = product(a[z, y, lo, :, 2 * block : 3 * block], p[z, y, hi]).astype(BF)
                ert[1, rows[y]] = product(a[z, y, hi, :, block : 2 * block], p[z, y, lo]).astype(BF)
            xv[1, z, i - 1] = product(pt[z, lo], ert[0])
            xv[0, z, i] = product(pt[z, hi], ert[1])

    def outer_columns(z):
        for y in range(depth):
            ert[2, rows[y]] = product(a[z, y, columns - 1, :, 2 * block : 3 * block], right[z, y]).astype(BF)
            ert[3, rows[y]] = product(a[z, y, 0, :, block : 2 * block], left[z, y]).astype(BF)
        xv[1, z, intervals - 1] = product(pt[z, columns - 1], ert[2])
        xv[0, z, 0] = product(pt[z, 0], ert[3])

    def x_sides(z):
        inside_columns(z)
        outer_columns(z)

    def outer_layer(side, z, k, ref, t):
        def step(j, _):
            for u in range(chunk):
                x = t * chunk + j * chunk + u
                for y in range(depth):
                    ert[u, rows[y]] = product(a[z, y, x, :, k * block : (k + 1) * block], ref[y, x]).astype(BF)
                coarse = product(pt[z, x], ert[u])
                before = ev[side, jnp.maximum(x - 1, 0)]
                ev[side, x] = coarse + jnp.where(column_begins(x) == 1, 0.0, before)
            return 0

        lax.fori_loop(0, 1, step, 0)

    S = [slice(k * width, (k + 1) * width) for k in range(5)]

    def layer_slots(z, i):
        end = jnp.clip(cuts[i + 1] - 1, 0, columns - 1)
        own = v[z, end, :, S[0]]
        zp = v[z, end, :, S[1]] if z < layers - 1 else ev[1, end]
        zm = v[z, end, :, S[2] if z < layers - 1 else S[1]] if z > 0 else ev[0, end]
        here, there = real(begins[z]), real(begins[z + 1])
        own = own + (1.0 - here) * zm + (1.0 - there) * zp
        return own, xv[0, z, i], xv[1, z, i], here * zm, there * zp

    def gathered(i, zs, wanted, slots):
        total = None
        for z in zs:
            w = real(jnp.where(group[z] == wanted, one, none))
            terms = layer_slots(z, i)
            terms = [terms[s] * w for s in slots]
            total = terms if total is None else [t + u for t, u in zip(total, terms)]
        return total

    p_copies[0].wait()
    for z in range(layers - 1):
        p_copies[z + 1].wait()
        for t in range(3):
            a_copies[z][t].wait()
        main(z)
    for t in range(3):
        a_copies[layers - 1][t].wait()

    @pl.when(has_left)
    def _():
        rightward.wait_recv()

    @pl.when(has_right)
    def _():
        leftward.wait_recv()

    for z in range(2):
        x_sides(z)
    for t in range(3):
        @pl.when(has_below)
        def _(t=t):
            up[t].wait_recv()
        outer_layer(0, 0, 5, below, t)
    for i in range(intervals):
        for s, term in enumerate(gathered(i, (0, 1), 0, (0, 1, 2, 4))):
            carry_out[i, :, S[s]] = term.astype(BF)

    @pl.when(has_below)
    def _():
        carry.start()

    main(layers - 1)
    for z in range(2, layers):
        x_sides(z)
    for i in range(intervals):
        for s, term in enumerate(gathered(i, range(layers - 1), 1, range(5))):
            done[0, i, :, S[s]] = term.astype(BF)
    first_out = pltpu.make_async_copy(done.at[0], out_hbm.at[0], o_sem.at[0])
    first_out.start()
    for t in range(3):
        @pl.when(has_above)
        def _(t=t):
            down[t].wait_recv()
        outer_layer(1, layers - 1, 6, above, t)
    for i in range(intervals):
        for s, term in enumerate(gathered(i, range(1, layers), 2, range(5))):
            last[i, :, S[s]] = term

    @pl.when(has_above)
    def _():
        carry.wait_recv()

    for i in range(intervals):
        for s, c in ((0, 0), (1, 1), (2, 2), (4, 3)):
            done[1, i, :, S[s]] = (last[i, :, S[s]] + carry_in[i, :, S[c]].astype(F32)).astype(BF)
        done[1, i, :, S[3]] = last[i, :, S[3]].astype(BF)
    second_out = pltpu.make_async_copy(done.at[1], out_hbm.at[1], o_sem.at[1])
    second_out.start()

    @pl.when(has_above)
    def _():
        for t in range(3):
            up[t].wait_send()

    @pl.when(has_below)
    def _():
        for t in range(3):
            down[t].wait_send()
        carry.wait_send()

    @pl.when(has_right)
    def _():
        rightward.wait_send()

    @pl.when(has_left)
    def _():
        leftward.wait_send()

    first_out.wait()
    second_out.wait()


def per_device(n_dom, n_grp, a_blocks, prolong, zagg, xlen):
    layers, depth, columns, block, width = prolong.shape
    intervals = xlen.shape[1]
    long = depth * block
    vm, dma = pltpu.VMEM, pltpu.SemaphoreType.DMA
    return pl.pallas_call(
        functools.partial(kernel, n_dom, n_grp),
        out_shape=jax.ShapeDtypeStruct((layers // 2, intervals, width, 5 * width), BF),
        in_specs=[pl.BlockSpec(memory_space=pltpu.SMEM)] * 2 + [pl.BlockSpec(memory_space=pl.ANY)] * 2,
        out_specs=pl.BlockSpec(memory_space=pl.ANY),
        scratch_shapes=[
            vm(a_blocks.shape, BF),
            vm(prolong.shape, BF),
            vm((layers, columns, width, long), BF),
            vm((UNROLL, long, 3 * width), BF),
            vm((4, long, width), BF),
            vm((layers, columns, width, 3 * width), F32),
            vm((2, columns, width, width), F32),
            vm((2, layers, intervals, width, width), F32),
            vm(prolong.shape[1:], BF),
            vm(prolong.shape[1:], BF),
            vm((layers, depth, block, width), BF),
            vm((layers, depth, block, width), BF),
            vm((intervals, width, 4 * width), BF),
            vm((intervals, width, 4 * width), BF),
            vm((intervals, width, 5 * width), F32),
            vm((layers // 2, intervals, width, 5 * width), BF),
            dma((layers, 3)), dma((layers,)), dma((2, 3)), dma((2, 3)),
            dma((2,)), dma((2,)), dma, dma, dma((2,)),
        ],
        compiler_params=pltpu.CompilerParams(
            collective_id=0, has_side_effects=True, vmem_limit_bytes=62 * 2**20
        ),
    )(zagg, xlen, a_blocks, prolong)


def solution(mesh):
    in_specs = (P("dom", None, "grp", None, None), P("dom", None, "grp", None, None), P(), P())
    return jax.shard_map(
        functools.partial(per_device, mesh.shape["dom"], mesh.shape["grp"]),
        mesh=mesh, in_specs=in_specs, out_specs=P("dom", "grp", None, None), check_vma=False,
    )
```

```python
import functools

import jax
import jax.numpy as jnp
from jax import lax
from jax.experimental import pallas as pl
from jax.experimental.pallas import tpu as pltpu
from jax.sharding import PartitionSpec as P

BF = jnp.bfloat16
F32 = jnp.float32
UNROLL = 4


def product(lhs, rhs):
    return jnp.dot(lhs, rhs, preferred_element_type=F32)


def kernel(
    n_dom, n_grp, zagg, xlen, a_hbm, p_hbm, done,
    a, p, pt, rt, ert, v, xv, below, above, left, right,
    carry_out, carry_in, last,
    a_sem, p_sem, z_send, z_recv, x_send, x_recv, c_send, c_recv,
):
    layers, depth, columns, block, width = p.shape
    chunk = columns // 3
    intervals = xlen.shape[1]
    dom, grp = lax.axis_index("dom"), lax.axis_index("grp")
    has_below, has_above = dom > 0, dom < n_dom - 1
    has_left, has_right = grp > 0, grp < n_grp - 1
    MESH = pl.DeviceIdType.MESH
    sides = (
        (has_below, (dom - 1, grp)),
        (has_above, (dom + 1, grp)),
        (has_left, (dom, grp - 1)),
        (has_right, (dom, grp + 1)),
    )

    def part(ref, z, third):
        return ref.at[z, :, pl.ds(third * chunk, chunk)]

    def a_copy(z, t):
        return pltpu.make_async_copy(part(a_hbm, z, t), part(a, z, t), a_sem.at[z, t])

    def p_copy(z, h):
        half = pl.ds(h * (columns // 2), columns // 2)
        return pltpu.make_async_copy(p_hbm.at[z, :, half], p.at[z, :, half], p_sem.at[z, h])

    order = [*range(1, layers - 1), 0, layers - 1]
    for z in range(3):
        p_copy(z, 0).start()
    a_copy(1, 0).start()
    for z in range(3):
        p_copy(z, 1).start()
    a_copy(1, 1).start()
    a_copy(1, 2).start()
    for z in range(3, layers):
        p_copy(z, 0).start()
        p_copy(z, 1).start()
    for z in order[1:]:
        for t in range(3):
            a_copy(z, t).start()

    barrier = pltpu.get_barrier_semaphore()
    for there, device in sides:
        @pl.when(there)
        def _(device=device):
            pl.semaphore_signal(barrier, inc=1, device_id=device, device_id_type=MESH)
    pl.semaphore_wait(barrier, sum(jnp.where(there, 1, 0).astype(jnp.int32) for there, _ in sides))

    def remote(src, dst, send, recv, device):
        return pltpu.make_async_remote_copy(
            src_ref=src, dst_ref=dst, send_sem=send, recv_sem=recv,
            device_id=device, device_id_type=MESH,
        )

    def thirds(ref, t):
        return ref.at[:, pl.ds(t * chunk, chunk)]

    def up_third(t):
        return remote(part(p_hbm, layers - 1, t), thirds(below, t), z_send.at[0, t], z_recv.at[0, t], (dom + 1, grp))

    def down_third(t):
        return remote(part(p_hbm, 0, t), thirds(above, t), z_send.at[1, t], z_recv.at[1, t], (dom - 1, grp))

    rightward = remote(p_hbm.at[:, :, columns - 1], left, x_send.at[0], x_recv.at[0], (dom, grp + 1))
    leftward = remote(p_hbm.at[:, :, 0], right, x_send.at[1], x_recv.at[1], (dom, grp - 1))
    carry = remote(carry_out, carry_in, c_send, c_recv, (dom - 1, grp))

    @pl.when(has_above)
    def _():
        for t in range(3):
            up_third(t).start()

    @pl.when(has_below)
    def _():
        for t in range(3):
            down_third(t).start()

    @pl.when(has_right)
    def _():
        rightward.start()

    @pl.when(has_left)
    def _():
        leftward.start()

    for there, ref in ((has_below, below), (has_above, above), (has_left, left), (has_right, right), (has_above, carry_in)):
        @pl.when(jnp.logical_not(there))
        def _(ref=ref):
            for first in range(ref.shape[0]):
                ref[first] = jnp.zeros(ref.shape[1:], ref.dtype)

    one, none = jnp.int32(1), jnp.int32(0)

    def begins_at(layer):
        at = dom * layers + layer
        inner = jnp.where(
            zagg[jnp.minimum(at, n_dom * layers - 1)] != zagg[jnp.maximum(at - 1, 0)], one, none
        )
        return jnp.where(jnp.logical_or(at == 0, at == n_dom * layers), one, inner)

    begins = [begins_at(layer) for layer in range(layers + 1)]
    group = [begins[0]]
    for layer in range(1, layers):
        group.append(group[-1] + begins[layer])
    cuts = [none]
    for i in range(intervals):
        cuts.append(cuts[-1] + xlen[grp, i])

    def column_begins(x):
        found = none
        for i in range(intervals):
            found = jnp.where(x == cuts[i], one, found)
        return jnp.where(x == columns, one, found)

    def real(flag):
        return flag.astype(F32)

    rows = [slice(y * block, (y + 1) * block) for y in range(depth)]

    def main(z):
        slots = 3 * width

        def over(y, x):
            return p[z + 1, y, x] if z < layers - 1 else above[y, x]

        def under(y, x):
            return p[z - 1, y, x] if z > 0 else below[y, x]

        def first(x, slot):
            same_xm = (1.0 - real(column_begins(x))).astype(BF)
            same_xp = (1.0 - real(column_begins(x + 1))).astype(BF)
            xm, xp = jnp.maximum(x - 1, 0), jnp.minimum(x + 1, columns - 1)
            zero = jnp.zeros((block, width), BF)
            for y in range(depth):
                stack = jnp.concatenate(
                    [
                        p[z, y, x],
                        p[z, y, xm] * same_xm,
                        p[z, y, xp] * same_xp,
                        p[z, y - 1, x] if y > 0 else zero,
                        p[z, y + 1, x] if y < depth - 1 else zero,
                    ],
                    axis=0,
                )
                rt[slot, rows[y], 0:width] = product(a[z, y, x, :, 0 : 5 * block], stack).astype(BF)
                rt[slot, rows[y], width : 2 * width] = product(
                    a[z, y, x, :, 6 * block : 7 * block], over(y, x)
                ).astype(BF)
                rt[slot, rows[y], 2 * width : slots] = product(
                    a[z, y, x, :, 5 * block : 6 * block], under(y, x)
                ).astype(BF)

        def second(x, slot):
            turned = jnp.concatenate([p[z, y, x] for y in range(depth)], axis=0).T
            pt[z, x] = turned
            coarse = product(turned, rt[slot, :, 0:slots])
            before = v[z, jnp.maximum(x - 1, 0), :, 0:slots]
            v[z, x, :, 0:slots] = coarse + jnp.where(column_begins(x) == 1, 0.0, before)

        def step(j, _):
            if z in order[:-2]:
                a_copy(z, j).wait()
            if z == order[0]:
                @pl.when(j == 1)
                def _():
                    for other in range(3):
                        p_copy(other, 1).wait()
            if z == 0:
                @pl.when(has_below)
                def _():
                    up_third(j).wait_recv()
            if z == layers - 1:
                @pl.when(has_above)
                def _():
                    down_third(j).wait_recv()
            for u in range(UNROLL):
                first(j * UNROLL + u, u)
                if u > 0:
                    second(j * UNROLL + u - 1, u - 1)
            second(j * UNROLL + UNROLL - 1, UNROLL - 1)
            return 0

        lax.fori_loop(0, columns // UNROLL, step, 0)

    def x_sides(z, at):
        for i in range(1, intervals):
            hi = jnp.clip(cuts[i], 1, columns - 1)
            lo = hi - 1
            for y in range(depth):
                ert[at, rows[y]] = product(a[z, y, lo, :, 2 * block : 3 * block], p[z, y, hi]).astype(BF)
                ert[at + 1, rows[y]] = product(a[z, y, hi, :, block : 2 * block], p[z, y, lo]).astype(BF)
            xv[1, z, i - 1] = product(pt[z, lo], ert[at])
            xv[0, z, i] = product(pt[z, hi], ert[at + 1])
            at += 2
        for y in range(depth):
            ert[at, rows[y]] = product(a[z, y, columns - 1, :, 2 * block : 3 * block], right[z, y]).astype(BF)
            ert[at + 1, rows[y]] = product(a[z, y, 0, :, block : 2 * block], left[z, y]).astype(BF)
        xv[1, z, intervals - 1] = product(pt[z, columns - 1], ert[at])
        xv[0, z, 0] = product(pt[z, 0], ert[at + 1])

    S = [slice(k * width, (k + 1) * width) for k in range(5)]

    def layer_slots(z, i):
        end = jnp.clip(cuts[i + 1] - 1, 0, columns - 1)
        own = v[z, end, :, S[0]]
        zp, zm = v[z, end, :, S[1]], v[z, end, :, S[2]]
        here, there = real(begins[z]), real(begins[z + 1])
        own = own + (1.0 - here) * zm + (1.0 - there) * zp
        return own, xv[0, z, i], xv[1, z, i], here * zm, there * zp

    def gathered(i, zs, wanted, slots):
        total = None
        for z in zs:
            w = real(jnp.where(group[z] == wanted, one, none))
            terms = layer_slots(z, i)
            terms = [terms[s] * w for s in slots]
            total = terms if total is None else [t + u for t, u in zip(total, terms)]
        return total

    for z in range(3):
        p_copy(z, 0).wait()
    main(1)
    for z in range(3, layers):
        p_copy(z, 0).wait()
        p_copy(z, 1).wait()
    for z in order[1:-2]:
        main(z)

    @pl.when(has_left)
    def _():
        rightward.wait_recv()

    @pl.when(has_right)
    def _():
        leftward.wait_recv()

    for t in range(3):
        a_copy(0, t).wait()
        a_copy(layers - 1, t).wait()
    for n, z in enumerate(order[:-2]):
        x_sides(z, 2 * intervals * n)
    main(0)
    x_sides(0, 0)
    for i in range(intervals):
        for s, term in enumerate(gathered(i, (0, 1), 0, (0, 1, 2, 4))):
            carry_out[i, :, S[s]] = term.astype(BF)

    @pl.when(has_below)
    def _():
        carry.start()

    main(layers - 1)
    x_sides(layers - 1, 0)
    for i in range(intervals):
        for s, term in enumerate(gathered(i, range(layers - 1), 1, range(5))):
            done[0, i, :, S[s]] = term.astype(BF)
    for i in range(intervals):
        for s, term in enumerate(gathered(i, range(1, layers), 2, range(5))):
            last[i, :, S[s]] = term

    @pl.when(has_above)
    def _():
        carry.wait_recv()

    for i in range(intervals):
        for s, c in ((0, 0), (1, 1), (2, 2), (4, 3)):
            done[1, i, :, S[s]] = (last[i, :, S[s]] + carry_in[i, :, S[c]].astype(F32)).astype(BF)
        done[1, i, :, S[3]] = last[i, :, S[3]].astype(BF)

    @pl.when(has_above)
    def _():
        for t in range(3):
            up_third(t).wait_send()

    @pl.when(has_below)
    def _():
        for t in range(3):
            down_third(t).wait_send()
        carry.wait_send()

    @pl.when(has_right)
    def _():
        rightward.wait_send()

    @pl.when(has_left)
    def _():
        leftward.wait_send()


def settle(made, out, sem):
    copies = [pltpu.make_async_copy(made.at[j, i], out.at[j, i], sem.at[j, i]) for j in range(2) for i in range(4)]
    for copy in copies:
        copy.start()
    for copy in copies:
        copy.wait()


def per_device(n_dom, n_grp, a_blocks, prolong, zagg, xlen):
    layers, depth, columns, block, width = prolong.shape
    intervals = xlen.shape[1]
    long = depth * block
    vm, dma = pltpu.VMEM, pltpu.SemaphoreType.DMA
    made = pl.pallas_call(
        functools.partial(kernel, n_dom, n_grp),
        out_shape=vm((layers // 2, intervals, width, 5 * width), BF),
        in_specs=[pl.BlockSpec(memory_space=pltpu.SMEM)] * 2 + [pl.BlockSpec(memory_space=pl.ANY)] * 2,
        out_specs=pl.BlockSpec(memory_space=pltpu.VMEM),
        scratch_shapes=[
            vm(a_blocks.shape, BF),
            vm(prolong.shape, BF),
            vm((layers, columns, width, long), BF),
            vm((UNROLL, long, 3 * width), BF),
            vm((4 * intervals, long, width), BF),
            vm((layers, columns, width, 3 * width), F32),
            vm((2, layers, intervals, width, width), F32),
            vm(prolong.shape[1:], BF),
            vm(prolong.shape[1:], BF),
            vm((layers, depth, block, width), BF),
            vm((layers, depth, block, width), BF),
            vm((intervals, width, 4 * width), BF),
            vm((intervals, width, 4 * width), BF),
            vm((intervals, width, 5 * width), F32),
            dma((layers, 3)), dma((layers, 2)), dma((2, 3)), dma((2, 3)),
            dma((2,)), dma((2,)), dma, dma,
        ],
        compiler_params=pltpu.CompilerParams(
            collective_id=0, has_side_effects=True, vmem_limit_bytes=60 * 2**20
        ),
    )(zagg, xlen, a_blocks, prolong)
    return pl.pallas_call(
        settle,
        out_shape=jax.ShapeDtypeStruct(made.shape, BF),
        in_specs=[pl.BlockSpec(memory_space=pl.ANY)],
        out_specs=pl.BlockSpec(memory_space=pl.ANY),
        scratch_shapes=[dma((2, 4))],
        compiler_params=pltpu.CompilerParams(vmem_limit_bytes=2**20),
    )(made)


def solution(mesh):
    in_specs = (P("dom", None, "grp", None, None), P("dom", None, "grp", None, None), P(), P())
    return jax.shard_map(
        functools.partial(per_device, mesh.shape["dom"], mesh.shape["grp"]),
        mesh=mesh, in_specs=in_specs, out_specs=P("dom", "grp", None, None), check_vma=False,
    )
```

```python
import functools

import jax
import jax.numpy as jnp
from jax import lax
from jax.experimental import pallas as pl
from jax.experimental.pallas import tpu as pltpu
from jax.sharding import PartitionSpec as P

BF = jnp.bfloat16
F32 = jnp.float32
UNROLL = 4


def product(lhs, rhs):
    return jnp.dot(lhs, rhs, preferred_element_type=F32)


def kernel(
    n_dom, n_grp, zagg, xlen, a_hbm, p_hbm, done,
    a, p, pt, v, xv, below, above, left, right,
    carry_out, carry_in, last, tile_out, tile_in, ev, late_out, late_in,
    a_sem, p_sem, z_send, z_recv, x_send, x_recv, c_send, c_recv, k_send, k_recv, l_send, l_recv,
):
    layers, depth, columns, block, width = p.shape
    chunk = columns // 3
    intervals = xlen.shape[1]
    dom, grp = lax.axis_index("dom"), lax.axis_index("grp")
    has_below, has_above = dom > 0, dom < n_dom - 1
    has_left, has_right = grp > 0, grp < n_grp - 1
    MESH = pl.DeviceIdType.MESH
    sides = (
        (has_below, (dom - 1, grp)),
        (has_above, (dom + 1, grp)),
        (has_left, (dom, grp - 1)),
        (has_right, (dom, grp + 1)),
    )

    def part(ref, z, third):
        return ref.at[z, :, pl.ds(third * chunk, chunk)]

    def a_copy(z, t):
        return pltpu.make_async_copy(part(a_hbm, z, t), part(a, z, t), a_sem.at[z, t])

    def p_copy(z, h):
        half = pl.ds(h * (columns // 2), columns // 2)
        return pltpu.make_async_copy(p_hbm.at[z, :, half], p.at[z, :, half], p_sem.at[z, h])

    order = [1, 0, *range(2, layers)]
    for z in range(3):
        p_copy(z, 0).start()
    a_copy(1, 0).start()

    barrier = pltpu.get_barrier_semaphore()
    for there, device in sides:
        @pl.when(there)
        def _(device=device):
            pl.semaphore_signal(barrier, inc=1, device_id=device, device_id_type=MESH)
    pl.semaphore_wait(barrier, sum(jnp.where(there, 1, 0).astype(jnp.int32) for there, _ in sides))

    def remote(src, dst, send, recv, device):
        return pltpu.make_async_remote_copy(
            src_ref=src, dst_ref=dst, send_sem=send, recv_sem=recv,
            device_id=device, device_id_type=MESH,
        )

    def thirds(ref, t):
        return ref.at[:, pl.ds(t * chunk, chunk)]

    def up_third(t):
        return remote(part(p_hbm, layers - 1, t), thirds(below, t), z_send.at[0, t], z_recv.at[0, t], (dom + 1, grp))

    def down_third(t):
        return remote(part(p_hbm, 0, t), thirds(above, t), z_send.at[1, t], z_recv.at[1, t], (dom - 1, grp))

    rightward = remote(p_hbm.at[:, :, columns - 1], left, x_send.at[0], x_recv.at[0], (dom, grp + 1))
    leftward = remote(p_hbm.at[:, :, 0], right, x_send.at[1], x_recv.at[1], (dom, grp - 1))
    carry = remote(carry_out, carry_in, c_send, c_recv, (dom - 1, grp))
    tiles = remote(tile_out, tile_in, k_send, k_recv, (dom + 1, grp))
    late = remote(late_out, late_in, l_send, l_recv, (dom - 1, grp))

    @pl.when(has_above)
    def _():
        for t in range(3):
            up_third(t).start()

    @pl.when(has_below)
    def _():
        for t in range(2):
            down_third(t).start()

    @pl.when(has_right)
    def _():
        rightward.start()

    @pl.when(has_left)
    def _():
        leftward.start()

    for there, ref in ((has_below, below), (has_above, above), (has_left, left), (has_right, right), (has_above, carry_in),
                       (has_above, late_in), (has_below, tile_in)):
        @pl.when(jnp.logical_not(there))
        def _(ref=ref):
            for first in range(ref.shape[0]):
                ref[first] = jnp.zeros(ref.shape[1:], ref.dtype)

    for y in range(depth):
        above[y, 2 * chunk :] = jnp.zeros((chunk, block, width), BF)

    one, none = jnp.int32(1), jnp.int32(0)

    def begins_at(layer):
        at = dom * layers + layer
        inner = jnp.where(
            zagg[jnp.minimum(at, n_dom * layers - 1)] != zagg[jnp.maximum(at - 1, 0)], one, none
        )
        return jnp.where(jnp.logical_or(at == 0, at == n_dom * layers), one, inner)

    begins = [begins_at(layer) for layer in range(layers + 1)]
    group = [begins[0]]
    for layer in range(1, layers):
        group.append(group[-1] + begins[layer])
    cuts = [none]
    for i in range(intervals):
        cuts.append(cuts[-1] + xlen[grp, i])

    def column_begins(x):
        found = none
        for i in range(intervals):
            found = jnp.where(x == cuts[i], one, found)
        return jnp.where(x == columns, one, found)

    def real(flag):
        return flag.astype(F32)

    rows = [slice(y * block, (y + 1) * block) for y in range(depth)]

    def main(z):
        slots = (3 if z > 0 else 2) * width

        def over(y, x):
            return p[z + 1, y, x] if z < layers - 1 else above[y, x]

        def first(x, slot):
            same_xm = (1.0 - real(column_begins(x))).astype(BF)
            same_xp = (1.0 - real(column_begins(x + 1))).astype(BF)
            xm, xp = jnp.maximum(x - 1, 0), jnp.minimum(x + 1, columns - 1)
            zero = jnp.zeros((block, width), BF)
            out = []
            for y in range(depth):
                stack = jnp.concatenate(
                    [
                        p[z, y, x],
                        p[z, y, xm] * same_xm,
                        p[z, y, xp] * same_xp,
                        p[z, y - 1, x] if y > 0 else zero,
                        p[z, y + 1, x] if y < depth - 1 else zero,
                    ],
                    axis=0,
                )
                parts = [
                    product(a[z, y, x, :, 0 : 5 * block], stack),
                    product(a[z, y, x, :, 6 * block : 7 * block], over(y, x)),
                ]
                if z > 0:
                    parts.append(product(a[z, y, x, :, 5 * block : 6 * block], p[z - 1, y, x]))
                out.append(jnp.concatenate(parts, axis=1).astype(BF))
            return jnp.concatenate(out, axis=0)

        def second(x, routed):
            turned = jnp.concatenate([p[z, y, x] for y in range(depth)], axis=0).T
            pt[z, x] = turned
            coarse = product(turned, routed)
            before = v[z, jnp.maximum(x - 1, 0), :, 0:slots]
            v[z, x, :, 0:slots] = coarse + jnp.where(column_begins(x) == 1, 0.0, before)

        def step(j, _):
            if z in order[:2]:
                a_copy(z, j).wait()
            if z == order[0]:
                @pl.when(j == 0)
                def _():
                    for other in range(3):
                        p_copy(other, 1).start()
                    a_copy(z, 1).start()
                    a_copy(z, 2).start()

                @pl.when(j == 1)
                def _():
                    for other in range(3):
                        p_copy(other, 1).wait()
                    for other in range(3, layers):
                        p_copy(other, 0).start()
                        p_copy(other, 1).start()
                    for t in range(3):
                        a_copy(order[1], t).start()

                @pl.when(j == 2)
                def _():
                    for other in order[2:]:
                        for t in range(3):
                            a_copy(other, t).start()
            if z == layers - 1:
                @pl.when(jnp.logical_and(has_above, j < 2))
                def _():
                    down_third(j).wait_recv()
            held = None
            for u in range(UNROLL):
                made = first(j * UNROLL + u, u)
                if u > 0:
                    second(j * UNROLL + u - 1, held)
                held = made
            second(j * UNROLL + UNROLL - 1, held)
            return 0

        lax.fori_loop(0, columns // UNROLL, step, 0)

    def x_sides(z):
        for i in range(1, intervals):
            hi = jnp.clip(cuts[i], 1, columns - 1)
            lo = hi - 1
            low = jnp.concatenate(
                [product(a[z, y, lo, :, 2 * block : 3 * block], p[z, y, hi]).astype(BF) for y in range(depth)], axis=0
            )
            high = jnp.concatenate(
                [product(a[z, y, hi, :, block : 2 * block], p[z, y, lo]).astype(BF) for y in range(depth)], axis=0
            )
            xv[1, z, i - 1] = product(pt[z, lo], low)
            xv[0, z, i] = product(pt[z, hi], high)
        low = jnp.concatenate(
            [product(a[z, y, columns - 1, :, 2 * block : 3 * block], right[z, y]).astype(BF) for y in range(depth)], axis=0
        )
        high = jnp.concatenate(
            [product(a[z, y, 0, :, block : 2 * block], left[z, y]).astype(BF) for y in range(depth)], axis=0
        )
        xv[1, z, intervals - 1] = product(pt[z, columns - 1], low)
        xv[0, z, 0] = product(pt[z, 0], high)

    def edge(t):
        @pl.when(has_below)
        def _():
            up_third(t).wait_recv()
        for x in range(t * chunk, (t + 1) * chunk):
            beside = jnp.concatenate(
                [product(a[0, y, x, :, 5 * block : 6 * block], below[y, x]).astype(BF) for y in range(depth)], axis=0
            )
            coarse = product(pt[0, x], beside)
            if x > 0:
                coarse = coarse + jnp.where(column_begins(x) == 1, 0.0, v[0, x - 1, :, 2 * width :])
            v[0, x, :, 2 * width :] = coarse

    def edge_of_below():
        @pl.when(has_below)
        def _():
            tiles.wait_recv()
        for u in range(chunk):
            x, half = 2 * chunk + u, u % 2 * block
            beside = jnp.concatenate(
                [product(tile_in[y, u // 2, :, half : half + block], p[0, y, x]).astype(BF) for y in range(depth)],
                axis=0,
            )
            turned = jnp.concatenate([below[y, x] for y in range(depth)], axis=0).T
            coarse = product(turned, beside)
            if u > 0:
                coarse = coarse + jnp.where(column_begins(x) == 1, 0.0, ev[u - 1])
            ev[u] = coarse

    S = [slice(k * width, (k + 1) * width) for k in range(5)]

    def layer_slots(z, i, early=False):
        end = jnp.clip(cuts[i + 1] - 1, 0, columns - 1)
        own = v[z, end, :, S[0]]
        zp, zm = v[z, end, :, S[1]], v[z, end, :, S[2]]
        here, there = real(begins[z]), real(begins[z + 1])
        if early and z == 0:
            return own + (1.0 - there) * zp, xv[0, z, i], xv[1, z, i], None, there * zp
        own = own + (1.0 - here) * zm + (1.0 - there) * zp
        return own, xv[0, z, i], xv[1, z, i], here * zm, there * zp

    def gathered(i, zs, wanted, slots, early=False):
        total = None
        for z in zs:
            w = real(jnp.where(group[z] == wanted, one, none))
            terms = layer_slots(z, i, early)
            terms = [terms[s] * w for s in slots]
            total = terms if total is None else [t + u for t, u in zip(total, terms)]
        return total

    for z in range(3):
        p_copy(z, 0).wait()
    main(1)
    main(0)
    for z in range(3, layers):
        p_copy(z, 0).wait()
        p_copy(z, 1).wait()

    for z in order[2:]:
        for t in range(3):
            a_copy(z, t).wait()
    for y in range(depth):
        for q in range(chunk // 2):
            x = 2 * chunk + 2 * q
            tile_out[y, q] = jnp.concatenate(
                [a[layers - 1, y, x + n, :, 6 * block : 7 * block] for n in range(2)], axis=1
            )

    @pl.when(has_above)
    def _():
        tiles.start()

    @pl.when(has_left)
    def _():
        rightward.wait_recv()

    @pl.when(has_right)
    def _():
        leftward.wait_recv()

    x_sides(0)
    x_sides(1)
    for i in range(intervals):
        for s, term in enumerate(gathered(i, (0, 1), 0, (0, 1, 2, 4), True)):
            carry_out[i, :, S[s]] = term.astype(BF)

    @pl.when(has_below)
    def _():
        carry.start()

    for z in order[2:-1]:
        main(z)
        x_sides(z)
    edge(0)
    edge(1)
    main(layers - 1)
    x_sides(layers - 1)
    for i in range(intervals):
        for s, term in enumerate(gathered(i, range(1, layers), 2, range(5))):
            last[i, :, S[s]] = term
    edge(2)
    edge_of_below()
    for i in range(intervals):
        end = jnp.clip(cuts[i + 1] - 1, 0, columns - 1)
        mine = (1.0 - real(begins[0])) * v[0, end, :, S[2]]
        theirs = ev[jnp.maximum(end - 2 * chunk, 0)]
        late_out[i] = (mine + real(jnp.where(end >= 2 * chunk, one, none)) * theirs).astype(BF)

    @pl.when(has_below)
    def _():
        late.start()

    for i in range(intervals):
        for s, term in enumerate(gathered(i, range(layers - 1), 1, range(5))):
            done[0, i, :, S[s]] = term.astype(BF)

    @pl.when(has_above)
    def _():
        carry.wait_recv()
        late.wait_recv()

    parted = real(begins[layers])
    for i in range(intervals):
        more = late_in[i].astype(F32)
        for s, c, w in ((0, 0, 1.0 - parted), (1, 1, None), (2, 2, None), (4, 3, parted)):
            term = last[i, :, S[s]] + carry_in[i, :, S[c]].astype(F32)
            done[1, i, :, S[s]] = (term if w is None else term + w * more).astype(BF)
        done[1, i, :, S[3]] = last[i, :, S[3]].astype(BF)

    @pl.when(has_above)
    def _():
        for t in range(3):
            up_third(t).wait_send()
        tiles.wait_send()

    @pl.when(has_below)
    def _():
        for t in range(2):
            down_third(t).wait_send()
        carry.wait_send()
        late.wait_send()

    @pl.when(has_right)
    def _():
        rightward.wait_send()

    @pl.when(has_left)
    def _():
        leftward.wait_send()


def settle(made, out, sem):
    copies = [pltpu.make_async_copy(made.at[j, i], out.at[j, i], sem.at[j, i]) for j in range(2) for i in range(4)]
    for copy in copies:
        copy.start()
    for copy in copies:
        copy.wait()


def per_device(n_dom, n_grp, a_blocks, prolong, zagg, xlen):
    layers, depth, columns, block, width = prolong.shape
    intervals = xlen.shape[1]
    long = depth * block
    vm, dma = pltpu.VMEM, pltpu.SemaphoreType.DMA
    made = pl.pallas_call(
        functools.partial(kernel, n_dom, n_grp),
        out_shape=vm((layers // 2, intervals, width, 5 * width), BF),
        in_specs=[pl.BlockSpec(memory_space=pltpu.SMEM)] * 2 + [pl.BlockSpec(memory_space=pl.ANY)] * 2,
        out_specs=pl.BlockSpec(memory_space=pltpu.VMEM),
        scratch_shapes=[
            vm(a_blocks.shape, BF),
            vm(prolong.shape, BF),
            vm((layers, columns, width, long), BF),
            vm((layers, columns, width, 3 * width), F32),
            vm((2, layers, intervals, width, width), F32),
            vm(prolong.shape[1:], BF),
            vm(prolong.shape[1:], BF),
            vm((layers, depth, block, width), BF),
            vm((layers, depth, block, width), BF),
            vm((intervals, width, 4 * width), BF),
            vm((intervals, width, 4 * width), BF),
            vm((intervals, width, 5 * width), F32),
            vm((depth, columns // 6, block, 2 * block), BF),
            vm((depth, columns // 6, block, 2 * block), BF),
            vm((columns // 3, width, width), F32),
            vm((intervals, width, width), BF),
            vm((intervals, width, width), BF),
            dma((layers, 3)), dma((layers, 2)), dma((2, 3)), dma((2, 3)),
            dma((2,)), dma((2,)), dma, dma, dma, dma, dma, dma,
        ],
        compiler_params=pltpu.CompilerParams(
            collective_id=0, has_side_effects=True, vmem_limit_bytes=60 * 2**20
        ),
    )(zagg, xlen, a_blocks, prolong)
    return pl.pallas_call(
        settle,
        out_shape=jax.ShapeDtypeStruct(made.shape, BF),
        in_specs=[pl.BlockSpec(memory_space=pl.ANY)],
        out_specs=pl.BlockSpec(memory_space=pl.ANY),
        scratch_shapes=[dma((2, 4))],
        compiler_params=pltpu.CompilerParams(vmem_limit_bytes=2**20),
    )(made)


def solution(mesh):
    in_specs = (P("dom", None, "grp", None, None), P("dom", None, "grp", None, None), P(), P())
    return jax.shard_map(
        functools.partial(per_device, mesh.shape["dom"], mesh.shape["grp"]),
        mesh=mesh, in_specs=in_specs, out_specs=P("dom", "grp", None, None), check_vma=False,
    )
```

```python
import functools

import jax
import jax.numpy as jnp
from jax import lax
from jax.experimental import pallas as pl
from jax.experimental.pallas import tpu as pltpu
from jax.sharding import PartitionSpec as P

BF = jnp.bfloat16
F32 = jnp.float32
UNROLL = 4


def product(lhs, rhs):
    return jnp.dot(lhs, rhs, preferred_element_type=F32)


def kernel(
    n_dom, n_grp, zagg, xlen, a_hbm, p_hbm, done,
    a, p, pt, v, xv, below, above, left, right,
    carry_out, carry_in, last, late_out, late_in,
    a_sem, p_sem, z_send, z_recv, x_send, x_recv, c_send, c_recv, l_send, l_recv,
):
    layers, depth, columns, block, width = p.shape
    chunk = columns // 3
    intervals = xlen.shape[1]
    dom, grp = lax.axis_index("dom"), lax.axis_index("grp")
    has_below, has_above = dom > 0, dom < n_dom - 1
    has_left, has_right = grp > 0, grp < n_grp - 1
    MESH = pl.DeviceIdType.MESH
    sides = (
        (has_below, (dom - 1, grp)),
        (has_above, (dom + 1, grp)),
        (has_left, (dom, grp - 1)),
        (has_right, (dom, grp + 1)),
    )

    def part(ref, z, third):
        return ref.at[z, :, pl.ds(third * chunk, chunk)]

    def a_copy(z, t):
        return pltpu.make_async_copy(part(a_hbm, z, t), part(a, z, t), a_sem.at[z, t])

    def p_copy(z, h):
        half = pl.ds(h * (columns // 2), columns // 2)
        return pltpu.make_async_copy(p_hbm.at[z, :, half], p.at[z, :, half], p_sem.at[z, h])

    order = [*range(1, layers - 1), 0, layers - 1]
    for z in range(3):
        p_copy(z, 0).start()
    a_copy(1, 0).start()

    barrier = pltpu.get_barrier_semaphore()
    for there, device in sides:
        @pl.when(there)
        def _(device=device):
            pl.semaphore_signal(barrier, inc=1, device_id=device, device_id_type=MESH)
    pl.semaphore_wait(barrier, sum(jnp.where(there, 1, 0).astype(jnp.int32) for there, _ in sides))

    def remote(src, dst, send, recv, device):
        return pltpu.make_async_remote_copy(
            src_ref=src, dst_ref=dst, send_sem=send, recv_sem=recv,
            device_id=device, device_id_type=MESH,
        )

    def thirds(ref, t):
        return ref.at[:, pl.ds(t * chunk, chunk)]

    def up_third(t):
        return remote(part(p_hbm, layers - 1, t), thirds(below, t), z_send.at[0, t], z_recv.at[0, t], (dom + 1, grp))

    def down_third(t):
        return remote(part(p_hbm, 0, t), thirds(above, t), z_send.at[1, t], z_recv.at[1, t], (dom - 1, grp))

    rightward = remote(p_hbm.at[:, :, columns - 1], left, x_send.at[0], x_recv.at[0], (dom, grp + 1))
    leftward = remote(p_hbm.at[:, :, 0], right, x_send.at[1], x_recv.at[1], (dom, grp - 1))
    carry = remote(carry_out, carry_in, c_send, c_recv, (dom - 1, grp))
    late = remote(late_out, late_in, l_send, l_recv, (dom - 1, grp))

    @pl.when(has_above)
    def _():
        for t in range(3):
            up_third(t).start()

    @pl.when(has_below)
    def _():
        for t in range(3):
            down_third(t).start()

    @pl.when(has_right)
    def _():
        rightward.start()

    @pl.when(has_left)
    def _():
        leftward.start()

    for there, ref in ((has_below, below), (has_above, above), (has_left, left), (has_right, right), (has_above, carry_in),
                       (has_above, late_in)):
        @pl.when(jnp.logical_not(there))
        def _(ref=ref):
            for first in range(ref.shape[0]):
                ref[first] = jnp.zeros(ref.shape[1:], ref.dtype)

    one, none = jnp.int32(1), jnp.int32(0)

    def begins_at(layer):
        at = dom * layers + layer
        inner = jnp.where(
            zagg[jnp.minimum(at, n_dom * layers - 1)] != zagg[jnp.maximum(at - 1, 0)], one, none
        )
        return jnp.where(jnp.logical_or(at == 0, at == n_dom * layers), one, inner)

    begins = [begins_at(layer) for layer in range(layers + 1)]
    group = [begins[0]]
    for layer in range(1, layers):
        group.append(group[-1] + begins[layer])
    cuts = [none]
    for i in range(intervals):
        cuts.append(cuts[-1] + xlen[grp, i])

    def column_begins(x):
        found = none
        for i in range(intervals):
            found = jnp.where(x == cuts[i], one, found)
        return jnp.where(x == columns, one, found)

    def real(flag):
        return flag.astype(F32)

    rows = [slice(y * block, (y + 1) * block) for y in range(depth)]

    def main(z, begin=0, end=3, low=True):
        slots = (3 if low else 2) * width

        def over(y, x):
            return p[z + 1, y, x] if z < layers - 1 else above[y, x]

        def under(y, x):
            return p[z - 1, y, x] if z > 0 else below[y, x]

        def first(x, slot):
            same_xm = (1.0 - real(column_begins(x))).astype(BF)
            same_xp = (1.0 - real(column_begins(x + 1))).astype(BF)
            xm, xp = jnp.maximum(x - 1, 0), jnp.minimum(x + 1, columns - 1)
            zero = jnp.zeros((block, width), BF)
            out = []
            for y in range(depth):
                stack = jnp.concatenate(
                    [
                        p[z, y, x],
                        p[z, y, xm] * same_xm,
                        p[z, y, xp] * same_xp,
                        p[z, y - 1, x] if y > 0 else zero,
                        p[z, y + 1, x] if y < depth - 1 else zero,
                    ],
                    axis=0,
                )
                parts = [
                    product(a[z, y, x, :, 0 : 5 * block], stack),
                    product(a[z, y, x, :, 6 * block : 7 * block], over(y, x)),
                ]
                if low:
                    parts.append(product(a[z, y, x, :, 5 * block : 6 * block], under(y, x)))
                out.append(jnp.concatenate(parts, axis=1).astype(BF))
            return jnp.concatenate(out, axis=0)

        def second(x, routed):
            turned = jnp.concatenate([p[z, y, x] for y in range(depth)], axis=0).T
            pt[z, x] = turned
            coarse = product(turned, routed)
            before = v[z, jnp.maximum(x - 1, 0), :, 0:slots]
            v[z, x, :, 0:slots] = coarse + jnp.where(column_begins(x) == 1, 0.0, before)

        def step(j, _):
            if z in order[:-2]:
                a_copy(z, j).wait()
            if z == order[0]:
                @pl.when(j == 0)
                def _():
                    for other in range(3):
                        p_copy(other, 1).start()
                    a_copy(z, 1).start()
                    a_copy(z, 2).start()

                @pl.when(j == 1)
                def _():
                    for other in range(3):
                        p_copy(other, 1).wait()
                    for other in range(3, layers):
                        p_copy(other, 0).start()
                        p_copy(other, 1).start()
                    for t in range(3):
                        a_copy(order[1], t).start()

                @pl.when(j == 2)
                def _():
                    for other in order[2:]:
                        for t in range(3):
                            a_copy(other, t).start()
            if z == 0 and low:
                @pl.when(has_below)
                def _():
                    up_third(j).wait_recv()
            if z == layers - 1:
                @pl.when(has_above)
                def _():
                    down_third(j).wait_recv()
            held = None
            for u in range(UNROLL):
                made = first(j * UNROLL + u, u)
                if u > 0:
                    second(j * UNROLL + u - 1, held)
                held = made
            second(j * UNROLL + UNROLL - 1, held)
            return 0

        lax.fori_loop(begin, end, step, 0)

    def x_sides(z):
        for i in range(1, intervals):
            hi = jnp.clip(cuts[i], 1, columns - 1)
            lo = hi - 1
            low = jnp.concatenate(
                [product(a[z, y, lo, :, 2 * block : 3 * block], p[z, y, hi]).astype(BF) for y in range(depth)], axis=0
            )
            high = jnp.concatenate(
                [product(a[z, y, hi, :, block : 2 * block], p[z, y, lo]).astype(BF) for y in range(depth)], axis=0
            )
            xv[1, z, i - 1] = product(pt[z, lo], low)
            xv[0, z, i] = product(pt[z, hi], high)
    def outer_sides(z):
        low = jnp.concatenate(
            [product(a[z, y, columns - 1, :, 2 * block : 3 * block], right[z, y]).astype(BF) for y in range(depth)], axis=0
        )
        high = jnp.concatenate(
            [product(a[z, y, 0, :, block : 2 * block], left[z, y]).astype(BF) for y in range(depth)], axis=0
        )
        xv[1, z, intervals - 1] = product(pt[z, columns - 1], low)
        xv[0, z, 0] = product(pt[z, 0], high)

    def edge(t):
        @pl.when(has_below)
        def _():
            up_third(t).wait_recv()
        for x in range(t * chunk, (t + 1) * chunk):
            beside = jnp.concatenate(
                [product(a[0, y, x, :, 5 * block : 6 * block], below[y, x]).astype(BF) for y in range(depth)], axis=0
            )
            coarse = product(pt[0, x], beside)
            if x > 0:
                coarse = coarse + jnp.where(column_begins(x) == 1, 0.0, v[0, x - 1, :, 2 * width :])
            v[0, x, :, 2 * width :] = coarse

    S = [slice(k * width, (k + 1) * width) for k in range(5)]

    def layer_slots(z, i, early=False):
        end = jnp.clip(cuts[i + 1] - 1, 0, columns - 1)
        own = v[z, end, :, S[0]]
        zp, zm = v[z, end, :, S[1]], v[z, end, :, S[2]]
        here, there = real(begins[z]), real(begins[z + 1])
        if early and z == 0:
            return own + (1.0 - there) * zp, xv[0, z, i], xv[1, z, i], None, there * zp
        own = own + (1.0 - here) * zm + (1.0 - there) * zp
        return own, xv[0, z, i], xv[1, z, i], here * zm, there * zp

    def gathered(i, zs, wanted, slots, early=False):
        total = None
        for z in zs:
            w = real(jnp.where(group[z] == wanted, one, none))
            terms = layer_slots(z, i, early)
            terms = [terms[s] * w for s in slots]
            total = terms if total is None else [t + u for t, u in zip(total, terms)]
        return total

    for z in range(3):
        p_copy(z, 0).wait()
    main(1)
    for z in range(3, layers):
        p_copy(z, 0).wait()
        p_copy(z, 1).wait()
    for z in order[1:-2]:
        main(z)

    for t in range(3):
        a_copy(0, t).wait()
        a_copy(layers - 1, t).wait()
    for z in order[:-2]:
        x_sides(z)
    main(0, 0, 2)
    main(0, 2, 3, False)
    x_sides(0)
    @pl.when(has_left)
    def _():
        rightward.wait_recv()

    @pl.when(has_right)
    def _():
        leftward.wait_recv()

    outer_sides(0)
    outer_sides(1)
    for i in range(intervals):
        for s, term in enumerate(gathered(i, (0, 1), 0, (0, 1, 2, 4), True)):
            carry_out[i, :, S[s]] = term.astype(BF)

    @pl.when(has_below)
    def _():
        carry.start()

    main(layers - 1, 0, 2)
    for z in order[1:-2]:
        outer_sides(z)
    edge(2)
    for i in range(intervals):
        end = jnp.clip(cuts[i + 1] - 1, 0, columns - 1)
        late_out[i] = ((1.0 - real(begins[0])) * v[0, end, :, S[2]]).astype(BF)

    @pl.when(has_below)
    def _():
        late.start()

    main(layers - 1, 2, 3)
    x_sides(layers - 1)
    outer_sides(layers - 1)
    for i in range(intervals):
        for s, term in enumerate(gathered(i, range(layers - 1), 1, range(5))):
            done[0, i, :, S[s]] = term.astype(BF)
    for i in range(intervals):
        for s, term in enumerate(gathered(i, range(1, layers), 2, range(5))):
            last[i, :, S[s]] = term

    @pl.when(has_above)
    def _():
        carry.wait_recv()
        late.wait_recv()

    for i in range(intervals):
        for s, c in ((0, 0), (1, 1), (2, 2), (4, 3)):
            term = last[i, :, S[s]] + carry_in[i, :, S[c]].astype(F32)
            done[1, i, :, S[s]] = (term + late_in[i].astype(F32) if s == 0 else term).astype(BF)
        done[1, i, :, S[3]] = last[i, :, S[3]].astype(BF)

    @pl.when(has_above)
    def _():
        for t in range(3):
            up_third(t).wait_send()

    @pl.when(has_below)
    def _():
        for t in range(3):
            down_third(t).wait_send()
        carry.wait_send()
        late.wait_send()

    @pl.when(has_right)
    def _():
        rightward.wait_send()

    @pl.when(has_left)
    def _():
        leftward.wait_send()


def settle(made, out, sem):
    copies = [pltpu.make_async_copy(made.at[j, i], out.at[j, i], sem.at[j, i]) for j in range(2) for i in range(4)]
    for copy in copies:
        copy.start()
    for copy in copies:
        copy.wait()


def per_device(n_dom, n_grp, a_blocks, prolong, zagg, xlen):
    layers, depth, columns, block, width = prolong.shape
    intervals = xlen.shape[1]
    long = depth * block
    vm, dma = pltpu.VMEM, pltpu.SemaphoreType.DMA
    made = pl.pallas_call(
        functools.partial(kernel, n_dom, n_grp),
        out_shape=vm((layers // 2, intervals, width, 5 * width), BF),
        in_specs=[pl.BlockSpec(memory_space=pltpu.SMEM)] * 2 + [pl.BlockSpec(memory_space=pl.ANY)] * 2,
        out_specs=pl.BlockSpec(memory_space=pltpu.VMEM),
        scratch_shapes=[
            vm(a_blocks.shape, BF),
            vm(prolong.shape, BF),
            vm((layers, columns, width, long), BF),
            vm((layers, columns, width, 3 * width), F32),
            vm((2, layers, intervals, width, width), F32),
            vm(prolong.shape[1:], BF),
            vm(prolong.shape[1:], BF),
            vm((layers, depth, block, width), BF),
            vm((layers, depth, block, width), BF),
            vm((intervals, width, 4 * width), BF),
            vm((intervals, width, 4 * width), BF),
            vm((intervals, width, 5 * width), F32),
            vm((intervals, width, width), BF),
            vm((intervals, width, width), BF),
            dma((layers, 3)), dma((layers, 2)), dma((2, 3)), dma((2, 3)),
            dma((2,)), dma((2,)), dma, dma, dma, dma,
        ],
        compiler_params=pltpu.CompilerParams(
            collective_id=0, has_side_effects=True, vmem_limit_bytes=60 * 2**20
        ),
    )(zagg, xlen, a_blocks, prolong)
    return pl.pallas_call(
        settle,
        out_shape=jax.ShapeDtypeStruct(made.shape, BF),
        in_specs=[pl.BlockSpec(memory_space=pl.ANY)],
        out_specs=pl.BlockSpec(memory_space=pl.ANY),
        scratch_shapes=[dma((2, 4))],
        compiler_params=pltpu.CompilerParams(vmem_limit_bytes=2**20),
    )(made)


def solution(mesh):
    in_specs = (P("dom", None, "grp", None, None), P("dom", None, "grp", None, None), P(), P())
    return jax.shard_map(
        functools.partial(per_device, mesh.shape["dom"], mesh.shape["grp"]),
        mesh=mesh, in_specs=in_specs, out_specs=P("dom", "grp", None, None), check_vma=False,
    )
```

```python
import functools

import jax
import jax.numpy as jnp
from jax import lax
from jax.experimental import pallas as pl
from jax.experimental.pallas import tpu as pltpu
from jax.sharding import PartitionSpec as P

BF = jnp.bfloat16
F32 = jnp.float32
UNROLL = 4


def product(lhs, rhs):
    return jnp.dot(lhs, rhs, preferred_element_type=F32)


def kernel(
    n_dom, n_grp, zagg, xlen, a_hbm, p_hbm, done,
    a, p, pt, v, xv, below, above, left, right,
    carry_out, carry_in, last, late_out, late_in,
    a_sem, p_sem, z_send, z_recv, x_send, x_recv, c_send, c_recv, l_send, l_recv,
):
    layers, depth, columns, block, width = p.shape
    chunk = columns // 3
    intervals = xlen.shape[1]
    dom, grp = lax.axis_index("dom"), lax.axis_index("grp")
    has_below, has_above = dom > 0, dom < n_dom - 1
    has_left, has_right = grp > 0, grp < n_grp - 1
    MESH = pl.DeviceIdType.MESH
    sides = (
        (has_below, (dom - 1, grp)),
        (has_above, (dom + 1, grp)),
        (has_left, (dom, grp - 1)),
        (has_right, (dom, grp + 1)),
    )

    def part(ref, z, third):
        return ref.at[z, :, pl.ds(third * chunk, chunk)]

    def a_copy(z, t):
        return pltpu.make_async_copy(part(a_hbm, z, t), part(a, z, t), a_sem.at[z, t])

    def p_copy(z, h):
        half = pl.ds(h * (columns // 2), columns // 2)
        return pltpu.make_async_copy(p_hbm.at[z, :, half], p.at[z, :, half], p_sem.at[z, h])

    order = [*range(1, layers - 1), 0, layers - 1]
    for z in range(3):
        p_copy(z, 0).start()
    a_copy(1, 0).start()

    barrier = pltpu.get_barrier_semaphore()
    for there, device in sides:
        @pl.when(there)
        def _(device=device):
            pl.semaphore_signal(barrier, inc=1, device_id=device, device_id_type=MESH)
    pl.semaphore_wait(barrier, sum(jnp.where(there, 1, 0).astype(jnp.int32) for there, _ in sides))

    def remote(src, dst, send, recv, device):
        return pltpu.make_async_remote_copy(
            src_ref=src, dst_ref=dst, send_sem=send, recv_sem=recv,
            device_id=device, device_id_type=MESH,
        )

    def thirds(ref, t):
        return ref.at[:, pl.ds(t * chunk, chunk)]

    def up_third(t):
        return remote(part(p_hbm, layers - 1, t), thirds(below, t), z_send.at[0, t], z_recv.at[0, t], (dom + 1, grp))

    def down_third(t):
        return remote(part(p_hbm, 0, t), thirds(above, t), z_send.at[1, t], z_recv.at[1, t], (dom - 1, grp))

    rightward = remote(p_hbm.at[:, :, columns - 1], left, x_send.at[0], x_recv.at[0], (dom, grp + 1))
    leftward = remote(p_hbm.at[:, :, 0], right, x_send.at[1], x_recv.at[1], (dom, grp - 1))
    carry = remote(carry_out, carry_in, c_send, c_recv, (dom - 1, grp))
    late = remote(late_out, late_in, l_send, l_recv, (dom - 1, grp))

    @pl.when(has_above)
    def _():
        for t in range(3):
            up_third(t).start()

    @pl.when(has_below)
    def _():
        for t in range(3):
            down_third(t).start()

    @pl.when(has_right)
    def _():
        rightward.start()

    @pl.when(has_left)
    def _():
        leftward.start()

    for there, ref in ((has_below, below), (has_above, above), (has_left, left), (has_right, right), (has_above, carry_in),
                       (has_above, late_in)):
        @pl.when(jnp.logical_not(there))
        def _(ref=ref):
            for first in range(ref.shape[0]):
                ref[first] = jnp.zeros(ref.shape[1:], ref.dtype)

    one, none = jnp.int32(1), jnp.int32(0)

    def begins_at(layer):
        at = dom * layers + layer
        inner = jnp.where(
            zagg[jnp.minimum(at, n_dom * layers - 1)] != zagg[jnp.maximum(at - 1, 0)], one, none
        )
        return jnp.where(jnp.logical_or(at == 0, at == n_dom * layers), one, inner)

    begins = [begins_at(layer) for layer in range(layers + 1)]
    group = [begins[0]]
    for layer in range(1, layers):
        group.append(group[-1] + begins[layer])
    cuts = [none]
    for i in range(intervals):
        cuts.append(cuts[-1] + xlen[grp, i])

    def column_begins(x):
        found = none
        for i in range(intervals):
            found = jnp.where(x == cuts[i], one, found)
        return jnp.where(x == columns, one, found)

    def real(flag):
        return flag.astype(F32)

    rows = [slice(y * block, (y + 1) * block) for y in range(depth)]

    def main(z, begin=0, end=3, low=True):
        slots = (3 if low else 2) * width

        def over(y, x):
            return p[z + 1, y, x] if z < layers - 1 else above[y, x]

        def under(y, x):
            return p[z - 1, y, x] if z > 0 else below[y, x]

        def first(x, slot):
            same_xm = (1.0 - real(column_begins(x))).astype(BF)
            same_xp = (1.0 - real(column_begins(x + 1))).astype(BF)
            xm, xp = jnp.maximum(x - 1, 0), jnp.minimum(x + 1, columns - 1)
            zero = jnp.zeros((block, width), BF)
            out = []
            for y in range(depth):
                stack = jnp.concatenate(
                    [
                        p[z, y, x],
                        p[z, y, xm] * same_xm,
                        p[z, y, xp] * same_xp,
                        p[z, y - 1, x] if y > 0 else zero,
                        p[z, y + 1, x] if y < depth - 1 else zero,
                    ],
                    axis=0,
                )
                parts = [
                    product(a[z, y, x, :, 0 : 5 * block], stack),
                    product(a[z, y, x, :, 6 * block : 7 * block], over(y, x)),
                ]
                if low:
                    parts.append(product(a[z, y, x, :, 5 * block : 6 * block], under(y, x)))
                out.append(jnp.concatenate(parts, axis=1).astype(BF))
            return jnp.concatenate(out, axis=0)

        def second(x, routed):
            turned = jnp.concatenate([p[z, y, x] for y in range(depth)], axis=0).T
            pt[z, x] = turned
            coarse = product(turned, routed)
            before = v[z, jnp.maximum(x - 1, 0), :, 0:slots]
            v[z, x, :, 0:slots] = coarse + jnp.where(column_begins(x) == 1, 0.0, before)

        def step(j, _):
            if z in order[:-2]:
                a_copy(z, j).wait()
            if z == order[0]:
                @pl.when(j == 0)
                def _():
                    for other in range(3):
                        p_copy(other, 1).start()
                    a_copy(z, 1).start()
                    a_copy(z, 2).start()

                @pl.when(j == 1)
                def _():
                    for other in range(3):
                        p_copy(other, 1).wait()
                    for other in range(3, layers):
                        p_copy(other, 0).start()
                        p_copy(other, 1).start()
                    for t in range(3):
                        a_copy(order[1], t).start()

                @pl.when(j == 2)
                def _():
                    for other in order[2:]:
                        for t in range(3):
                            a_copy(other, t).start()
            if z == 0 and low:
                @pl.when(has_below)
                def _():
                    up_third(j).wait_recv()
            if z == layers - 1:
                @pl.when(has_above)
                def _():
                    down_third(j).wait_recv()
            held = None
            for u in range(UNROLL):
                made = first(j * UNROLL + u, u)
                if u > 0:
                    second(j * UNROLL + u - 1, held)
                held = made
            second(j * UNROLL + UNROLL - 1, held)
            return 0

        lax.fori_loop(begin, end, step, 0)

    def x_sides(z):
        for i in range(1, intervals):
            hi = jnp.clip(cuts[i], 1, columns - 1)
            lo = hi - 1
            low = jnp.concatenate(
                [product(a[z, y, lo, :, 2 * block : 3 * block], p[z, y, hi]).astype(BF) for y in range(depth)], axis=0
            )
            high = jnp.concatenate(
                [product(a[z, y, hi, :, block : 2 * block], p[z, y, lo]).astype(BF) for y in range(depth)], axis=0
            )
            xv[1, z, i - 1] = product(pt[z, lo], low)
            xv[0, z, i] = product(pt[z, hi], high)
    def outer_sides(z):
        low = jnp.concatenate(
            [product(a[z, y, columns - 1, :, 2 * block : 3 * block], right[z, y]).astype(BF) for y in range(depth)], axis=0
        )
        high = jnp.concatenate(
            [product(a[z, y, 0, :, block : 2 * block], left[z, y]).astype(BF) for y in range(depth)], axis=0
        )
        xv[1, z, intervals - 1] = product(pt[z, columns - 1], low)
        xv[0, z, 0] = product(pt[z, 0], high)

    def edge(t):
        @pl.when(has_below)
        def _():
            up_third(t).wait_recv()
        for x in range(t * chunk, (t + 1) * chunk):
            beside = jnp.concatenate(
                [product(a[0, y, x, :, 5 * block : 6 * block], below[y, x]).astype(BF) for y in range(depth)], axis=0
            )
            coarse = product(pt[0, x], beside)
            if x > 0:
                coarse = coarse + jnp.where(column_begins(x) == 1, 0.0, v[0, x - 1, :, 2 * width :])
            v[0, x, :, 2 * width :] = coarse

    S = [slice(k * width, (k + 1) * width) for k in range(5)]

    def layer_slots(z, i, early=False):
        end = jnp.clip(cuts[i + 1] - 1, 0, columns - 1)
        own = v[z, end, :, S[0]]
        zp, zm = v[z, end, :, S[1]], v[z, end, :, S[2]]
        here, there = real(begins[z]), real(begins[z + 1])
        if early and z == 0:
            return own + (1.0 - there) * zp, xv[0, z, i], xv[1, z, i], None, there * zp
        own = own + (1.0 - here) * zm + (1.0 - there) * zp
        return own, xv[0, z, i], xv[1, z, i], here * zm, there * zp

    def gathered(i, zs, wanted, slots, early=False):
        total = None
        for z in zs:
            w = real(jnp.where(group[z] == wanted, one, none))
            terms = layer_slots(z, i, early)
            terms = [terms[s] * w for s in slots]
            total = terms if total is None else [t + u for t, u in zip(total, terms)]
        return total

    for z in range(3):
        p_copy(z, 0).wait()
    main(1)
    for z in range(3, layers):
        p_copy(z, 0).wait()
        p_copy(z, 1).wait()
    for z in order[1:-2]:
        main(z)

    for t in range(3):
        a_copy(0, t).wait()
        a_copy(layers - 1, t).wait()
    x_sides(1)
    main(0, 0, 2)
    main(0, 2, 3, False)
    x_sides(0)
    sent = [(s, i) for s in range(4) for i in range(intervals) if (s, i) not in ((1, 0), (2, intervals - 1))]
    tile_of = {key: n for n, key in enumerate(sent)}
    for i in range(intervals):
        for s, term in enumerate(gathered(i, (0, 1), 0, (0, 1, 2, 4), True)):
            if (s, i) in tile_of:
                carry_out[tile_of[s, i]] = term.astype(BF)

    @pl.when(has_below)
    def _():
        carry.start()

    for z in order[1:-2]:
        x_sides(z)
    @pl.when(has_left)
    def _():
        rightward.wait_recv()

    @pl.when(has_right)
    def _():
        leftward.wait_recv()

    for z in range(layers - 1):
        outer_sides(z)
    edge(2)
    for i in range(intervals):
        end = jnp.clip(cuts[i + 1] - 1, 0, columns - 1)
        late_out[i] = ((1.0 - real(begins[0])) * v[0, end, :, S[2]]).astype(BF)

    for side, at in ((0, 0), (1, intervals - 1)):
        late_out[intervals + side] = sum(
            real(jnp.where(group[z] == 0, one, none)) * xv[side, z, at] for z in range(2)
        ).astype(BF)

    @pl.when(has_below)
    def _():
        late.start()

    main(layers - 1)
    x_sides(layers - 1)
    outer_sides(layers - 1)
    for i in range(intervals):
        for s, term in enumerate(gathered(i, range(layers - 1), 1, range(5))):
            done[0, i, :, S[s]] = term.astype(BF)
    for i in range(intervals):
        for s, term in enumerate(gathered(i, range(1, layers), 2, range(5))):
            last[i, :, S[s]] = term

    @pl.when(has_above)
    def _():
        carry.wait_recv()
        late.wait_recv()

    for i in range(intervals):
        for s, c in ((0, 0), (1, 1), (2, 2), (4, 3)):
            term = last[i, :, S[s]]
            if (c, i) in tile_of:
                term = term + carry_in[tile_of[c, i]].astype(F32)
            if s == 0:
                term = term + late_in[i].astype(F32)
            if s == 1 and i == 0:
                term = term + late_in[intervals].astype(F32)
            if s == 2 and i == intervals - 1:
                term = term + late_in[intervals + 1].astype(F32)
            done[1, i, :, S[s]] = term.astype(BF)
        done[1, i, :, S[3]] = last[i, :, S[3]].astype(BF)

    @pl.when(has_above)
    def _():
        for t in range(3):
            up_third(t).wait_send()

    @pl.when(has_below)
    def _():
        for t in range(3):
            down_third(t).wait_send()
        carry.wait_send()
        late.wait_send()

    @pl.when(has_right)
    def _():
        rightward.wait_send()

    @pl.when(has_left)
    def _():
        leftward.wait_send()


def settle(made, out, sem):
    copies = [pltpu.make_async_copy(made.at[j, i], out.at[j, i], sem.at[j, i]) for j in range(2) for i in range(4)]
    for copy in copies:
        copy.start()
    for copy in copies:
        copy.wait()


def per_device(n_dom, n_grp, a_blocks, prolong, zagg, xlen):
    layers, depth, columns, block, width = prolong.shape
    intervals = xlen.shape[1]
    long = depth * block
    vm, dma = pltpu.VMEM, pltpu.SemaphoreType.DMA
    made = pl.pallas_call(
        functools.partial(kernel, n_dom, n_grp),
        out_shape=vm((layers // 2, intervals, width, 5 * width), BF),
        in_specs=[pl.BlockSpec(memory_space=pltpu.SMEM)] * 2 + [pl.BlockSpec(memory_space=pl.ANY)] * 2,
        out_specs=pl.BlockSpec(memory_space=pltpu.VMEM),
        scratch_shapes=[
            vm(a_blocks.shape, BF),
            vm(prolong.shape, BF),
            vm((layers, columns, width, long), BF),
            vm((layers, columns, width, 3 * width), F32),
            vm((2, layers, intervals, width, width), F32),
            vm(prolong.shape[1:], BF),
            vm(prolong.shape[1:], BF),
            vm((layers, depth, block, width), BF),
            vm((layers, depth, block, width), BF),
            vm((4 * intervals - 2, width, width), BF),
            vm((4 * intervals - 2, width, width), BF),
            vm((intervals, width, 5 * width), F32),
            vm((intervals + 2, width, width), BF),
            vm((intervals + 2, width, width), BF),
            dma((layers, 3)), dma((layers, 2)), dma((2, 3)), dma((2, 3)),
            dma((2,)), dma((2,)), dma, dma, dma, dma,
        ],
        compiler_params=pltpu.CompilerParams(
            collective_id=0, has_side_effects=True, vmem_limit_bytes=60 * 2**20
        ),
    )(zagg, xlen, a_blocks, prolong)
    return pl.pallas_call(
        settle,
        out_shape=jax.ShapeDtypeStruct(made.shape, BF),
        in_specs=[pl.BlockSpec(memory_space=pl.ANY)],
        out_specs=pl.BlockSpec(memory_space=pl.ANY),
        scratch_shapes=[dma((2, 4))],
        compiler_params=pltpu.CompilerParams(vmem_limit_bytes=2**20),
    )(made)


def solution(mesh):
    in_specs = (P("dom", None, "grp", None, None), P("dom", None, "grp", None, None), P(), P())
    return jax.shard_map(
        functools.partial(per_device, mesh.shape["dom"], mesh.shape["grp"]),
        mesh=mesh, in_specs=in_specs, out_specs=P("dom", "grp", None, None), check_vma=False,
    )
```
